256 devices in a mesh: row: 8 (over x_lo, y), col: 32 (over x_hi, z, core).
Axes of the slice: x: 4 (x_hi: 2, x_lo: 2; x = x_hi * 2 + x_lo), y: 4, z: 8, core: 2. Of those that a mesh axis runs over, the one named last changes fastest.
Arguments:
- sigma_sep: float32 [4096, 4096], P('col', 'row')
- factor_one: float32 [16384, 4096], P('col', 'row'), may hold values from -0.109375 to 0.109375
- inverse_one: float32 [128, 128, 128], P('col')
- list_one: int32 [128, 24], P('col'), may hold values from -1 to 31, as said below
- factor_two: float32 [16384, 4096], P('col', 'row'), may hold values from -0.109375 to 0.109375
- factor_link: float32 [128, 128, 128], P('col'), may hold values from -0.5 to 0.5
- inverse_two: float32 [128, 128, 128], P('col')
- list_two: int32 [128, 24], P('col'), may hold values from -1 to 31, as said below
Outputs:
- cross_one: float32 [16384, 4096], P('col', 'row')
- diag_one: float32 [128, 128, 128], P('col')
- cross_two: float32 [16384, 4096], P('col', 'row')
- link_two: float32 [128, 128, 128], P('col')
- diag_two: float32 [128, 128, 128], P('col')
The draws below stay inside these ranges and needn't reach their ends.
Inputs may be any that keep to these rules, and one draw needn't show every extreme that they name: Each row of list_one names distinct separator tiles followed by -1 entries; some row names 24 tiles and some row fewer. Row s of list_two keeps some of the tiles of row s of list_one at their places and holds -1 elsewhere.
All inputs are finite; a program needn't handle non-finite values.
Results may differ from the reference program's by a relative error of at most 0.000076.
Values sent between devices are 32-bit elements; how exact they have to be, the bound alone decides.
A program may use at most 192 MiB of HBM per device.

```python
import math
import jax
import jax.numpy as jnp
from jax import lax

TILE = 128
SEP = 32
SEP_ROWS = 4096
LISTED = 24
SUPER = 128


def draw_sigma_sep(key, part):
    key = jax.random.fold_in(key, 1)
    noise_key, diag_key = jax.random.split(key)
    order = SEP * TILE
    noise = jax.random.normal(noise_key, (order, order), jnp.float32)
    spread = 1.0
    diagonal = jnp.exp(jax.random.uniform(diag_key, (order,), jnp.float32, 0.0, math.log(4.0)))
    symmetric = (noise + noise.T) * (spread / math.sqrt(2.0 * order))
    ident = jnp.arange(order)[:, None] == jnp.arange(order)[None, :]
    return jnp.where(ident, diagonal[:, None], symmetric)


def lower_shape(key, diagonal):
    noise = jax.random.normal(key, (SUPER, TILE, TILE), jnp.float32) * (0.5 / math.sqrt(TILE))
    row_ids = jnp.arange(TILE)[:, None]
    col_ids = jnp.arange(TILE)[None, :]
    strict = (row_ids > col_ids)[None]
    ident = (row_ids == col_ids)[None]
    return jnp.where(ident, diagonal[:, :, None], jnp.where(strict, noise, 0.0))


def draw_inverse_one(key, part):
    key = jax.random.fold_in(key, 2)
    noise_key, diag_key = jax.random.split(key)
    diagonal = jnp.exp(jax.random.uniform(diag_key, (SUPER, TILE), jnp.float32, math.log(0.7), math.log(1.5)))
    return lower_shape(noise_key, diagonal)


def draw_inverse_two(key, part):
    key = jax.random.fold_in(key, 4)
    noise_key, diag_key = jax.random.split(key)
    diagonal = jnp.exp(jax.random.uniform(diag_key, (SUPER, TILE), jnp.float32, math.log(0.7), math.log(1.5)))
    return lower_shape(noise_key, diagonal)


def base_lists(key):
    key = jax.random.fold_in(key, 11)
    score_key, count_key, pick_key = jax.random.split(key, 3)
    full_row = jax.random.randint(pick_key, (), 0, SUPER)
    short_row = (full_row + 1) % SUPER
    row_ids = jnp.arange(SUPER, dtype=jnp.int32)
    tile_ids = jnp.arange(SEP, dtype=jnp.int32)
    scores = jax.random.randint(score_key, (SUPER, SEP), 0, 1 << 20) * SEP + tile_ids[None, :]
    forced = (row_ids[:, None] == full_row) & (tile_ids[None, :] == SEP - 1)
    scores = jnp.where(forced, -1, scores)
    order = jnp.argsort(scores, axis=1, stable=True).astype(jnp.int32)
    chosen = order[:, :LISTED]
    counts = jax.random.randint(count_key, (SUPER,), max(1, LISTED // 3), LISTED + 1)
    counts = jnp.where(row_ids == full_row, LISTED, counts)
    counts = jnp.where(row_ids == short_row, max(1, LISTED // 3), counts)
    keep = jnp.arange(LISTED, dtype=jnp.int32)[None, :] < counts[:, None]
    return (jnp.where(keep, chosen, -1).astype(jnp.int32), full_row)


def draw_list_one(key, part):
    shared, full_row = base_lists(key)
    return shared


def draw_list_two(key, part):
    shared, full_row = base_lists(key)
    key = jax.random.fold_in(key, 5)
    dropped = jax.random.randint(key, (SUPER, LISTED), 0, 4) == 0
    dropped = dropped & (jnp.arange(SUPER, dtype=jnp.int32)[:, None] != full_row)
    return jnp.where(dropped, -1, shared).astype(jnp.int32)


def steps_of(stream_key, dims, pieces, least, largest):
    loudness, own = 1.0, jax.random.fold_in(stream_key, 6)
    for axis_at, shards_of in pieces:
        steps = jnp.exp(jax.random.uniform(jax.random.fold_in(own, axis_at), (shards_of,), jnp.float32, least / len(pieces), largest / len(pieces)))
        loudness = loudness * jnp.repeat(steps, dims[axis_at] // shards_of).reshape([-1 if axis == axis_at else 1 for axis in range(len(dims))])
    return loudness


def centred(key, shape, deviation, limit, pieces=(), kind=jnp.bfloat16):
    factor_of = steps_of(key, shape, pieces, -0.22, 0.18) if pieces else 1.0
    array = jax.random.normal(key, shape, jnp.float32) * deviation * factor_of
    return jnp.minimum(jnp.maximum(array, -limit), limit).astype(kind)


def setup_inputs(seed: int = 0) -> dict:
    key_of = jax.random.split(jax.random.key(seed), 9)
    sigma_sep = draw_sigma_sep(jax.random.fold_in(key_of[8], 71), 0)
    factor_one = centred(key_of[1], (SUPER * TILE, SEP_ROWS), (TILE * LISTED) ** -0.5, 0.109375, ((0, 32), (1, 8)), jnp.float32)
    inverse_one = draw_inverse_one(jax.random.fold_in(key_of[8], 71), 0)
    list_one = draw_list_one(jax.random.fold_in(key_of[8], 71), 0)
    factor_two = centred(key_of[4], (SUPER * TILE, SEP_ROWS), (TILE * LISTED) ** -0.5, 0.109375, ((0, 32), (1, 8)), jnp.float32)
    factor_link = centred(key_of[5], (SUPER, TILE, TILE), TILE ** -0.5, 0.5, ((0, 32),), jnp.float32)
    inverse_two = draw_inverse_two(jax.random.fold_in(key_of[8], 71), 0)
    list_two = draw_list_two(jax.random.fold_in(key_of[8], 71), 0)
    return dict(sigma_sep=sigma_sep, factor_one=factor_one, inverse_one=inverse_one, list_one=list_one, factor_two=factor_two, factor_link=factor_link, inverse_two=inverse_two, list_two=list_two)


highest = lax.Precision.HIGHEST


def tile_hits(lists):
    tile_ids = jnp.arange(SEP, dtype=jnp.int32)
    marks = jnp.sum((lists[:, :, None] == tile_ids[None, None, :]).astype(jnp.float32), axis=1)
    return jnp.repeat(marks, TILE, axis=1)[:, None, :]


def reference(sigma_sep, factor_one, inverse_one, list_one, factor_two, factor_link, inverse_two, list_two):
    hits_one = tile_hits(list_one)
    hits_two = tile_hits(list_two)
    lower_one = factor_one.reshape(SUPER, TILE, SEP_ROWS) * hits_one
    upper_one = jnp.einsum('sij,sia->sja', inverse_one, lower_one, precision=highest)
    prod_one = jnp.einsum('sja,ab->sjb', upper_one, sigma_sep, precision=highest)
    cross_one = -(hits_one * prod_one)
    gram_one = jnp.einsum('sij,sik->sjk', inverse_one, inverse_one, precision=highest)
    diag_one = gram_one + jnp.einsum('sja,ska->sjk', upper_one, prod_one, precision=highest)
    lower_two = factor_two.reshape(SUPER, TILE, SEP_ROWS) * hits_two
    upper_two = jnp.einsum('sij,sia->sja', inverse_two, lower_two, precision=highest)
    link_upper = jnp.einsum('sij,spi->sjp', inverse_two, factor_link, precision=highest)
    prod_two = jnp.einsum('sja,ab->sjb', upper_two, sigma_sep, precision=highest)
    prod_two = prod_two + jnp.einsum('sjp,spa->sja', link_upper, cross_one, precision=highest)
    cross_two = -(hits_two * prod_two)
    link_prod = jnp.einsum('spa,ska->spk', cross_one, upper_two, precision=highest)
    link_prod = link_prod + jnp.einsum('spq,skq->spk', diag_one, link_upper, precision=highest)
    gram_two = jnp.einsum('sij,sik->sjk', inverse_two, inverse_two, precision=highest)
    diag_two = gram_two + jnp.einsum('sja,ska->sjk', upper_two, prod_two, precision=highest)
    diag_two = diag_two + jnp.einsum('sjp,spk->sjk', link_upper, link_prod, precision=highest)
    return (cross_one.reshape(SUPER * TILE, SEP_ROWS), diag_one,
            cross_two.reshape(SUPER * TILE, SEP_ROWS), -link_prod, diag_two)
```

```python
import functools

import jax
import jax.numpy as jnp
from jax import lax
from jax.experimental import pallas as pl
from jax.experimental.pallas import tpu as pltpu
from jax.sharding import PartitionSpec as P

TILE = 128
MESH = pl.DeviceIdType.MESH
F32 = jnp.float32
BF16 = jnp.bfloat16
WIDE = 512
SUPERS = 4
CHUNKS = 8


def split(x):
    high = x.astype(BF16)
    low = (x - high.astype(F32)).astype(BF16)
    return high, low


def dot3(a, b, ca, cb):
    ah, al = split(a)
    bh, bl = split(b)
    dg = lambda u, v: lax.dot_general(u, v, (((ca,), (cb,)), ((), ())), preferred_element_type=F32)
    return dg(ah, bh) + (dg(ah, bl) + dg(al, bh))


def kernel(
    sig, f1, i1, n1, f2, fl, i2, n2,
    c1, d1, c2, l2, d2,
    H, A, As, B, Bh, Bl, Cs, Cr, Po, P1, R1, G1, P2, R2, G2, LU,
    as_s, as_r, af_s, af_r, bx_s, bx_r, bz_s, bz_r, bc_s, bc_r, c_s, c_r, r1_s, r1_r, g1_s, g1_r, r2_s, r2_r, g2_s, g2_r,
):
    row = lax.axis_index("row")
    col = lax.axis_index("col")
    xl, y = row // 4, row % 4
    xh, z, c = col // 16, (col // 2) % 8, col % 2
    sends = []

    def remote(src, dst, ss, rs, dev):
        return pltpu.make_async_remote_copy(
            src_ref=src, dst_ref=dst, send_sem=ss, recv_sem=rs, device_id=dev, device_id_type=MESH
        )

    def start(*args):
        copy = remote(*args)
        copy.start()
        sends.append(copy)

    def arrived(ref, sem):
        pltpu.make_async_copy(ref, ref, sem).wait()

    right, left = (xl * 4 + (y + 1) % 4, col), (xl * 4 + (y + 3) % 4, col)
    pair = ((1 - xl) * 4 + y, col)
    up, down = (row, xh * 16 + ((z + 1) % 8) * 2 + c), (row, xh * 16 + ((z + 7) % 8) * 2 + c)
    twin = (row, xh * 16 + z * 2 + (1 - c))
    other_col = (1 - xh) * 16 + z * 2 + c
    peers = [((row + i) % 8, col) for i in range(1, 8)]
    barrier = pltpu.get_barrier_semaphore()
    for dev in peers + [up, down, twin, (row, other_col), ((1 - xl) * 4 + y, other_col)]:
        pl.semaphore_signal(barrier, inc=1, device_id=dev, device_id_type=MESH)

    for level, lists in enumerate((n1, n2)):
        for t in range(4):
            match = jnp.where(lists[...] == row * 4 + t, 1.0, 0.0).astype(F32)
            mark = jnp.sum(match, axis=1, keepdims=True)
            H[level, :, t * TILE:(t + 1) * TILE] = jnp.broadcast_to(mark, (SUPERS, TILE))

    def hits(level, s):
        return H[level, s:s + 1, :]

    def upper(q):
        level, s = q // SUPERS, q % SUPERS
        f, inv = ((f1, i1), (f2, i2))[level]
        masked = f[s * TILE:(s + 1) * TILE, :] * hits(level, s)
        A[y, q * TILE:(q + 1) * TILE, :] = dot3(inv[s].T, masked, 1, 0)

    def a_block(slot, first, count):
        return A.at[slot, pl.ds(first, count), :]

    def a_send(q):
        for d, dev in enumerate((right, left)):
            ref = a_block(y, q * TILE, TILE)
            start(ref, ref, as_s.at[d, q], as_r.at[d, q], dev)

    def a_forward(q):
        for d, dev in enumerate((right, left)):
            slot = (y + (3, 1)[d]) % 4
            arrived(a_block(slot, q * TILE, TILE), as_r.at[d, q])
            ref = a_block(slot, q * TILE + d * 64, 64)
            start(ref, ref, af_s.at[d, q], af_r.at[d, q], dev)

    def a_ready(q):
        for d in range(2):
            arrived(a_block((y + 2) % 4, q * TILE + d * 64, 64), af_r.at[d, q])
        for k in range(4):
            high, low = split(A[k, q * TILE:(q + 1) * TILE, :])
            As[q, 0:TILE, k * WIDE:(k + 1) * WIDE] = high
            As[q, TILE:2 * TILE, k * WIDE:(k + 1) * WIDE] = low

    def b_rows(k, zs, core, h):
        first = pl.multiple_of(((zs + 8) % 8 * 2 + core) * TILE + h * 64, 64)
        return B.at[(1 - xl, xl)[k], pl.ds(first, 64), :]

    def b_spread(k):
        for h in range(2):
            src = sig.at[pl.ds(h * 64, 64), :]
            dst = B.at[xl, pl.ds(pl.multiple_of((z * 2 + c) * TILE + h * 64, 64), 64), :]

            def out(i, colt):
                return remote(src, dst, bx_s.at[i, h], bx_r.at[k, h], (xh * 4 + y, colt))

            if k == 0:
                @pl.when(xl != xh)
                def _():
                    out(0, z * 2 + c).start()
                    out(1, 16 + z * 2 + c).start()
            else:
                @pl.when(xl == xh)
                def _():
                    pltpu.make_async_copy(src, dst, bx_r.at[k, h]).start()
                    out(0, other_col).start()

    def b_spread_done():
        for h in range(2):
            src = sig.at[pl.ds(h * 64, 64), :]
            remote(src, src, bx_s.at[0, h], bx_r.at[0, h], pair).wait_send()

            @pl.when(xl != xh)
            def _():
                remote(src, src, bx_s.at[1, h], bx_r.at[0, h], pair).wait_send()

    def b_pass(k, d, s, h):
        ref = b_rows(k, z + (-s, s)[d], c, h)
        start(ref, ref, bz_s.at[k, d, s, h], bz_r.at[k, d, s, h], (up, down)[d])

    def b_twin(k, d, s, h):
        ref = b_rows(k, z + (-s, s)[d], c, h)
        start(ref, ref, bc_s.at[k, d, s, h], bc_r.at[k, d, s, h], twin)

    def b_home(k):
        for h in range(2):
            arrived(b_rows(k, z, c, h), bx_r.at[k, h])
            b_pass(k, 0, 0, h)
            b_pass(k, 1, 0, h)
            b_twin(k, 0, 0, h)

    def b_step(k, s, h):
        for d in range(2):
            arrived(b_rows(k, z + (-s, s)[d], c, h), bz_r.at[k, d, s - 1, h])
            if s < 3 or h == d:
                b_pass(k, d, s, h)
            b_twin(k, d, s, h)

    def b_last(k):
        for d in range(2):
            arrived(b_rows(k, z + 4, c, d), bz_r.at[k, d, 3, d])
            b_twin(k, d, 4, d)
        for h in range(2):
            arrived(b_rows(k, z, 1 - c, h), bc_r.at[k, 0, 0, h])
            for d in range(2):
                for s in range(1, 4):
                    arrived(b_rows(k, z + (-s, s)[d], 1 - c, h), bc_r.at[k, d, s, h])
            arrived(b_rows(k, z + 4, 1 - c, h), bc_r.at[k, h, 4, h])
        which = (1 - xl, xl)[k]

        def cut(i, carry):
            rows = pl.ds(pl.multiple_of(i * TILE, TILE), TILE)
            high, low = split(B[which, rows, :])
            Bh[which, rows, :] = high
            Bl[which, rows, :] = low
            return carry

        lax.fori_loop(0, 16, cut, 0)

    def product(q, k, out):
        which = (1 - xl, xl)[k]
        total = None
        for step in range(4):
            ks = slice(step * WIDE, (step + 1) * WIDE)
            both = jnp.dot(As[q, :, ks], Bh[which, ks, :], preferred_element_type=F32)
            rest = jnp.dot(As[q, 0:TILE, ks], Bl[which, ks, :], preferred_element_type=F32)
            term = both[0:TILE] + (both[TILE:2 * TILE] + rest)
            total = term if total is None else total + term
        out[q, :, :] = total

    def c_send(q):
        product(q, 0, Cs)
        start(Cs.at[q], Cr.at[q], c_s.at[q], c_r.at[q], pair)

    def own_upper(q):
        return A[y, q * TILE:(q + 1) * TILE, :]

    def finish_one(s):
        arrived(Cr.at[s], c_r.at[s])
        prod = Po[s] + Cr[s]
        cross = -(hits(0, s) * prod)
        c1[s * TILE:(s + 1) * TILE, :] = cross
        P1[:, s] = dot3(own_upper(s), prod, 1, 1).reshape(8, 16, TILE)
        P1[:, SUPERS + s] = dot3(cross, own_upper(SUPERS + s), 1, 1).reshape(8, 16, TILE)

    def finish_two(s):
        q = SUPERS + s
        arrived(Cr.at[q], c_r.at[q])
        prod = Po[q] + Cr[q] + dot3(LU[s], c1[s * TILE:(s + 1) * TILE, :], 1, 0)
        c2[s * TILE:(s + 1) * TILE, :] = -(hits(1, s) * prod)
        P2[:, s] = dot3(own_upper(q), prod, 1, 1).reshape(8, 16, TILE)

    def scatter(part, got, ss, rs):
        for i, dev in enumerate(peers):
            start(part.at[dev[0]], got.at[i], ss.at[i], rs.at[i], dev)

    def gather(part, got, whole, waits, ss, rs):
        total = part[row]
        for i in range(7):
            arrived(got.at[i], waits.at[i])
            total = total + got[i]
        whole[row] = total
        for i, dev in enumerate(peers):
            start(whole.at[row], whole.at[row], ss.at[i], rs.at[i], dev)

    def gathered(whole, waits):
        for i in range(7):
            arrived(whole.at[(row + 7 - i) % 8], waits.at[i])

    def side():
        for s in range(SUPERS):
            t1, t2 = i1[s].T, i2[s].T
            LU[s] = dot3(t2, fl[s], 1, 1)
            d1[s] = dot3(t1, t1, 1, 1)
            d2[s] = dot3(t2, t2, 1, 1)

    def tiles_one():
        gathered(G1, g1_r)
        for s in range(SUPERS):
            diag = d1[s] + G1[:, s].reshape(TILE, TILE)
            d1[s] = diag
            link = G1[:, SUPERS + s].reshape(TILE, TILE) + dot3(diag, LU[s], 1, 1)
            l2[s] = -link
            d2[s] = d2[s] + dot3(LU[s], link, 1, 0)

    upper(0)
    pl.semaphore_wait(barrier, 12)
    b_spread(0)
    a_send(0)
    upper(1)
    a_send(1)
    upper(2)
    a_send(2)
    upper(3)
    b_home(0)
    b_spread(1)
    upper(4)
    upper(5)
    a_forward(0)
    a_send(3)
    b_step(0, 1, 0)
    b_step(0, 1, 1)
    upper(6)
    upper(7)
    a_forward(1)
    a_send(4)
    b_step(0, 2, 0)
    b_step(0, 2, 1)
    side()
    b_step(0, 3, 0)
    a_forward(2)
    a_send(5)
    b_step(0, 3, 1)
    b_home(1)
    b_last(0)
    a_ready(0)
    c_send(0)
    a_forward(3)
    a_send(6)
    a_ready(1)
    b_step(1, 1, 0)
    c_send(1)
    b_step(1, 1, 1)
    a_ready(2)
    c_send(2)
    b_step(1, 2, 0)
    a_forward(4)
    a_send(7)
    b_step(1, 2, 1)
    a_ready(3)
    c_send(3)
    b_step(1, 3, 0)
    b_step(1, 3, 1)
    a_ready(4)
    c_send(4)
    a_forward(5)
    b_last(1)
    product(0, 1, Po)
    a_ready(5)
    c_send(5)
    finish_one(0)
    product(1, 1, Po)
    finish_one(1)
    a_forward(6)
    product(2, 1, Po)
    finish_one(2)
    a_ready(6)
    c_send(6)
    product(3, 1, Po)
    finish_one(3)
    scatter(P1, R1, r1_s, r1_r)
    a_forward(7)
    product(4, 1, Po)
    finish_two(0)
    product(5, 1, Po)
    finish_two(1)
    gather(P1, R1, G1, r1_r, g1_s, g1_r)
    a_ready(7)
    c_send(7)
    product(6, 1, Po)
    product(7, 1, Po)
    finish_two(2)
    tiles_one()
    finish_two(3)
    scatter(P2, R2, r2_s, r2_r)
    gather(P2, R2, G2, r2_r, g2_s, g2_r)
    gathered(G2, g2_r)
    for s in range(SUPERS):
        d2[s] = d2[s] + G2[:, s].reshape(TILE, TILE)
    b_spread_done()
    for copy in sends:
        copy.wait_send()


def local(
    sigma_sep, factor_one, inverse_one, list_one, factor_two, factor_link, inverse_two, list_two
):
    vmem = pl.BlockSpec(memory_space=pltpu.VMEM)
    wide = jax.ShapeDtypeStruct((SUPERS * TILE, WIDE), F32)
    tiles = jax.ShapeDtypeStruct((SUPERS, TILE, TILE), F32)
    dma = pltpu.SemaphoreType.DMA
    return pl.pallas_call(
        kernel,
        out_shape=(wide, tiles, wide, tiles, tiles),
        in_specs=[vmem] * 8,
        out_specs=(vmem,) * 5,
        scratch_shapes=[
            pltpu.VMEM((2, SUPERS, WIDE), F32),
            pltpu.VMEM((4, CHUNKS * TILE, WIDE), F32),
            pltpu.VMEM((CHUNKS, 2 * TILE, 4 * WIDE), BF16),
            pltpu.VMEM((2, 4 * WIDE, WIDE), F32),
            pltpu.VMEM((2, 4 * WIDE, WIDE), BF16),
            pltpu.VMEM((2, 4 * WIDE, WIDE), BF16),
            pltpu.VMEM((CHUNKS, TILE, WIDE), F32),
            pltpu.VMEM((CHUNKS, TILE, WIDE), F32),
            pltpu.VMEM((CHUNKS, TILE, WIDE), F32),
            pltpu.VMEM((8, 2 * SUPERS, 16, TILE), F32),
            pltpu.VMEM((7, 2 * SUPERS, 16, TILE), F32),
            pltpu.VMEM((8, 2 * SUPERS, 16, TILE), F32),
            pltpu.VMEM((8, SUPERS, 16, TILE), F32),
            pltpu.VMEM((7, SUPERS, 16, TILE), F32),
            pltpu.VMEM((8, SUPERS, 16, TILE), F32),
            pltpu.VMEM((SUPERS, TILE, TILE), F32),
            dma((2, CHUNKS)), dma((2, CHUNKS)), dma((2, CHUNKS)), dma((2, CHUNKS)),
            dma((2, 2)), dma((2, 2)),
            dma((2, 2, 4, 2)), dma((2, 2, 4, 2)),
            dma((2, 2, 5, 2)), dma((2, 2, 5, 2)),
            dma((CHUNKS,)), dma((CHUNKS,)),
            dma((7,)), dma((7,)), dma((7,)), dma((7,)),
            dma((7,)), dma((7,)), dma((7,)), dma((7,)),
        ],
        compiler_params=pltpu.CompilerParams(
            collective_id=0, has_side_effects=True, vmem_limit_bytes=60 * 2**20
        ),
        cost_estimate=pl.CostEstimate(
            flops=13_000_000_000, bytes_accessed=8_000_000, transcendentals=0
        ),
    )(sigma_sep, factor_one, inverse_one, list_one, factor_two, factor_link, inverse_two, list_two)


def solution(mesh):
    return jax.shard_map(
        local,
        mesh=mesh,
        in_specs=(
            P("col", "row"),
            P("col", "row"),
            P("col", None, None),
            P("col", None),
            P("col", "row"),
            P("col", None, None),
            P("col", None, None),
            P("col", None),
        ),
        out_specs=(
            P("col", "row"),
            P("col", None, None),
            P("col", "row"),
            P("col", None, None),
            P("col", None, None),
        ),
        check_vma=False,
    )
```

```python
import functools

import jax
import jax.numpy as jnp
from jax import lax
from jax.experimental import pallas as pl
from jax.experimental.pallas import tpu as pltpu
from jax.sharding import PartitionSpec as P

TILE = 128
MESH = pl.DeviceIdType.MESH
F32 = jnp.float32
BF16 = jnp.bfloat16
WIDE = 512
SUPERS = 4
CHUNKS = 8


def split(x):
    high = x.astype(BF16)
    low = (x - high.astype(F32)).astype(BF16)
    return high, low


def dot3(a, b, ca, cb):
    ah, al = split(a)
    bh, bl = split(b)
    dg = lambda u, v: lax.dot_general(u, v, (((ca,), (cb,)), ((), ())), preferred_element_type=F32)
    return dg(ah, bh) + (dg(ah, bl) + dg(al, bh))


def kernel(
    sig, f1, i1, n1, f2, fl, i2, n2,
    o1, od1, o2, ol2, od2,
    c1, d1, c2, l2, d2, F, Up, H, A, As, B, Bh, Bl, Cs, Cr, Po, P1, X1, Y1, G1, P2, R2, G2, P3, R3, G3, LU,
    as_s, as_r, af_s, af_r, bx_s, bx_r, bz_s, bz_r, bc_s, bc_r, c_s, c_r, x1_s, x1_r, y1_s, y1_r, g1_s, g1_r, r2_s, r2_r, g2_s, g2_r,
    r3_s, r3_r, g3_s, g3_r, f_r, u_s, u_r, o_s,
):
    row = lax.axis_index("row")
    col = lax.axis_index("col")
    xl, y = row // 4, row % 4
    xh, z, c = col // 16, (col // 2) % 8, col % 2
    sends = []

    def remote(src, dst, ss, rs, dev):
        return pltpu.make_async_remote_copy(
            src_ref=src, dst_ref=dst, send_sem=ss, recv_sem=rs, device_id=dev, device_id_type=MESH
        )

    def start(*args):
        copy = remote(*args)
        copy.start()
        sends.append(copy)

    def arrived(ref, sem):
        pltpu.make_async_copy(ref, ref, sem).wait()

    right, left = (xl * 4 + (y + 1) % 4, col), (xl * 4 + (y + 3) % 4, col)
    pair = ((1 - xl) * 4 + y, col)
    up, down = (row, xh * 16 + ((z + 1) % 8) * 2 + c), (row, xh * 16 + ((z + 7) % 8) * 2 + c)
    twin = (row, xh * 16 + z * 2 + (1 - c))
    other_col = (1 - xh) * 16 + z * 2 + c
    peers = [((row + i) % 8, col) for i in range(1, 8)]
    barrier = pltpu.get_barrier_semaphore()
    for dev in peers + [up, down, twin, (row, other_col), ((1 - xl) * 4 + y, other_col)]:
        pl.semaphore_signal(barrier, inc=1, device_id=dev, device_id_type=MESH)

    def load(q):
        rows = pl.ds(q % SUPERS * TILE, TILE)
        return pltpu.make_async_copy((f1, f2)[q // SUPERS].at[rows, :], F.at[q], f_r.at[q])

    for q in range(CHUNKS):
        load(q).start()

    for level, lists in enumerate((n1, n2)):
        for t in range(4):
            match = jnp.where(lists[...] == row * 4 + t, 1.0, 0.0).astype(F32)
            mark = jnp.sum(match, axis=1, keepdims=True)
            H[level, :, t * TILE:(t + 1) * TILE] = jnp.broadcast_to(mark, (SUPERS, TILE))

    def hits(level, s):
        return H[level, s:s + 1, :]

    def upper(q):
        level, s = q // SUPERS, q % SUPERS
        inv = (i1, i2)[level]
        load(q).wait()
        masked = F[q, :, :] * hits(level, s)
        A[y, q * TILE:(q + 1) * TILE, :] = dot3(inv[s].T, masked, 1, 0)

    def a_block(slot, first, count):
        return A.at[slot, pl.ds(first, count), :]

    def a_send(q):
        for d, dev in enumerate((right, left)):
            ref = a_block(y, q * TILE, TILE)
            start(ref, ref, as_s.at[d, q], as_r.at[d, q], dev)

    def a_forward(q):
        for d, dev in enumerate((right, left)):
            slot = (y + (3, 1)[d]) % 4
            arrived(a_block(slot, q * TILE, TILE), as_r.at[d, q])
            ref = a_block(slot, q * TILE + d * 64, 64)
            start(ref, ref, af_s.at[d, q], af_r.at[d, q], dev)

    def a_ready(q):
        for d in range(2):
            arrived(a_block((y + 2) % 4, q * TILE + d * 64, 64), af_r.at[d, q])
        for k in range(4):
            high, low = split(A[k, q * TILE:(q + 1) * TILE, :])
            As[q, 0:TILE, k * WIDE:(k + 1) * WIDE] = high
            As[q, TILE:2 * TILE, k * WIDE:(k + 1) * WIDE] = low

    def b_rows(k, zs, core, h):
        first = pl.multiple_of(((zs + 8) % 8 * 2 + core) * TILE + h * 64, 64)
        return B.at[(1 - xl, xl)[k], pl.ds(first, 64), :]

    def b_spread(k):
        for h in range(2):
            src = sig.at[pl.ds(h * 64, 64), :]
            dst = B.at[xl, pl.ds(pl.multiple_of((z * 2 + c) * TILE + h * 64, 64), 64), :]

            def out(i, colt):
                return remote(src, dst, bx_s.at[i, h], bx_r.at[k, h], (xh * 4 + y, colt))

            if k == 0:
                @pl.when(xl != xh)
                def _():
                    out(0, z * 2 + c).start()
                    out(1, 16 + z * 2 + c).start()
            else:
                @pl.when(xl == xh)
                def _():
                    pltpu.make_async_copy(src, dst, bx_r.at[k, h]).start()
                    out(0, other_col).start()

    def b_spread_done():
        for h in range(2):
            src = sig.at[pl.ds(h * 64, 64), :]
            remote(src, src, bx_s.at[0, h], bx_r.at[0, h], pair).wait_send()

            @pl.when(xl != xh)
            def _():
                remote(src, src, bx_s.at[1, h], bx_r.at[0, h], pair).wait_send()

    def b_pass(k, d, s, h):
        ref = b_rows(k, z + (-s, s)[d], c, h)
        start(ref, ref, bz_s.at[k, d, s, h], bz_r.at[k, d, s, h], (up, down)[d])

    def b_twin(k, d, s, h):
        ref = b_rows(k, z + (-s, s)[d], c, h)
        start(ref, ref, bc_s.at[k, d, s, h], bc_r.at[k, d, s, h], twin)

    def b_home(k):
        for h in range(2):
            arrived(b_rows(k, z, c, h), bx_r.at[k, h])
            b_pass(k, 0, 0, h)
            b_pass(k, 1, 0, h)
            b_twin(k, 0, 0, h)

    def b_step(k, s, h):
        for d in range(2):
            arrived(b_rows(k, z + (-s, s)[d], c, h), bz_r.at[k, d, s - 1, h])
            if s < 3 or h == d:
                b_pass(k, d, s, h)
            b_twin(k, d, s, h)

    def b_last(k):
        for d in range(2):
            arrived(b_rows(k, z + 4, c, d), bz_r.at[k, d, 3, d])
            b_twin(k, d, 4, d)
        for h in range(2):
            arrived(b_rows(k, z, 1 - c, h), bc_r.at[k, 0, 0, h])
            for d in range(2):
                for s in range(1, 4):
                    arrived(b_rows(k, z + (-s, s)[d], 1 - c, h), bc_r.at[k, d, s, h])
            arrived(b_rows(k, z + 4, 1 - c, h), bc_r.at[k, h, 4, h])
        which = (1 - xl, xl)[k]

        def cut(i, carry):
            rows = pl.ds(pl.multiple_of(i * TILE, TILE), TILE)
            high, low = split(B[which, rows, :])
            Bh[which, rows, :] = high
            Bl[which, rows, :] = low
            return carry

        lax.fori_loop(0, 16, cut, 0)

    def product(q, k, out):
        which = (1 - xl, xl)[k]
        total = None
        for step in range(4):
            ks = slice(step * WIDE, (step + 1) * WIDE)
            both = jnp.dot(As[q, :, ks], Bh[which, ks, :], preferred_element_type=F32)
            rest = jnp.dot(As[q, 0:TILE, ks], Bl[which, ks, :], preferred_element_type=F32)
            term = both[0:TILE] + (both[TILE:2 * TILE] + rest)
            total = term if total is None else total + term
        out[q, :, :] = total

    def c_send(q):
        product(q, 0, Cs)
        start(Cs.at[q], Cr.at[q], c_s.at[q], c_r.at[q], pair)

    def own_upper(q):
        return A[y, q * TILE:(q + 1) * TILE, :]

    def finish_one(s):
        arrived(Cr.at[s], c_r.at[s])
        prod = Po[s] + Cr[s]
        cross = -(hits(0, s) * prod)
        c1[s * TILE:(s + 1) * TILE, :] = cross
        P1[0, s] = dot3(own_upper(s), prod, 1, 1)
        P1[1, s] = dot3(cross, own_upper(SUPERS + s), 1, 1)

    def linked(s):
        q = SUPERS + s
        Po[q] = Po[q] + dot3(LU[s], c1[s * TILE:(s + 1) * TILE, :], 1, 0)

    def cross_two(s):
        q = SUPERS + s
        arrived(Cr.at[q], c_r.at[q])
        prod = Po[q] + Cr[q]
        c2[s * TILE:(s + 1) * TILE, :] = -(hits(1, s) * prod)
        return prod

    def finish_two(s):
        linked(s)
        P2[:, s] = dot3(own_upper(SUPERS + s), cross_two(s), 1, 1).reshape(8, 16, TILE)

    def send_upper(i):
        start(A.at[y, pl.ds((6 + i) * TILE, TILE), :], Up.at[i], u_s.at[i], u_r.at[i], pair)

    def last_two(i):
        linked(2 + i)
        arrived(Up.at[i], u_r.at[i])
        part = dot3(own_upper(6 + i), Po[6 + i], 1, 1) + dot3(Up[i], Cs[6 + i], 1, 1)
        P3[:, i] = part.reshape(8, 16, TILE)

    def one_pair():
        start(P1.at[1 - xl], X1, x1_s, x1_r, pair)

    def one_ring():
        arrived(X1, x1_r)
        for s in range(SUPERS):
            X1[s] = X1[s] + P1[xl, s]
        for i in range(3):
            to = (y + i + 1) % 4
            start(X1.at[to], Y1.at[i], y1_s.at[i], y1_r.at[i], (xl * 4 + to, col))

    def one_all():
        total = X1[y]
        for i in range(3):
            arrived(Y1.at[i], y1_r.at[i])
            total = total + Y1[i]
        G1[xl, y] = total
        for i, dev in enumerate(peers):
            start(G1.at[xl, y], G1.at[xl, y], g1_s.at[i], g1_r.at[i], dev)

    def scatter(part, got, ss, rs):
        for i, dev in enumerate(peers):
            start(part.at[dev[0]], got.at[i], ss.at[i], rs.at[i], dev)

    def gather(part, got, whole, waits, ss, rs):
        total = part[row]
        for i in range(7):
            arrived(got.at[i], waits.at[i])
            total = total + got[i]
        whole[row] = total
        for i, dev in enumerate(peers):
            start(whole.at[row], whole.at[row], ss.at[i], rs.at[i], dev)

    def gathered(whole, waits):
        for i in range(7):
            arrived(whole.at[(row + 7 - i) % 8], waits.at[i])

    def side():
        for s in range(SUPERS):
            t1, t2 = i1[s].T, i2[s].T
            LU[s] = dot3(t2, fl[s], 1, 1)
            d1[s] = dot3(t1, t1, 1, 1)
            d2[s] = dot3(t2, t2, 1, 1)

    def tiles_one():
        for i in range(7):
            sender = (row + 7 - i) % 8
            arrived(G1.at[sender // 4, sender % 4], g1_r.at[i])
        for s in range(SUPERS):
            diag = d1[s] + G1[0, s]
            d1[s] = diag
            link = G1[1, s] + dot3(diag, LU[s], 1, 1)
            l2[s] = -link
            d2[s] = d2[s] + dot3(LU[s], link, 1, 0)

    def write(i, src, dst):
        return pltpu.make_async_copy(src, dst, o_s.at[i])

    upper(0)
    pl.semaphore_wait(barrier, 12)
    a_send(0)
    b_spread(0)
    upper(1)
    a_send(1)
    upper(2)
    a_send(2)
    upper(3)
    b_home(0)
    b_spread(1)
    upper(7)
    send_upper(1)
    upper(4)
    a_forward(0)
    a_send(3)
    b_step(0, 1, 0)
    b_step(0, 1, 1)
    upper(5)
    upper(6)
    send_upper(0)
    a_forward(1)
    a_send(4)
    b_step(0, 2, 0)
    b_step(0, 2, 1)
    side()
    b_step(0, 3, 0)
    a_forward(2)
    a_send(5)
    b_step(0, 3, 1)
    b_home(1)
    b_last(0)
    a_ready(0)
    c_send(0)
    a_forward(3)
    a_send(6)
    a_ready(1)
    b_step(1, 1, 0)
    c_send(1)
    b_step(1, 1, 1)
    a_ready(2)
    c_send(2)
    b_step(1, 2, 0)
    a_forward(4)
    a_send(7)
    b_step(1, 2, 1)
    a_ready(3)
    c_send(3)
    b_step(1, 3, 0)
    b_step(1, 3, 1)
    a_ready(4)
    c_send(4)
    a_forward(5)
    b_last(1)
    product(0, 1, Po)
    a_ready(5)
    c_send(5)
    finish_one(0)
    product(1, 1, Po)
    finish_one(1)
    a_forward(6)
    product(2, 1, Po)
    finish_one(2)
    product(3, 1, Po)
    finish_one(3)
    one_pair()
    write(0, c1, o1).start()
    a_ready(6)
    c_send(6)
    product(4, 1, Po)
    finish_two(0)
    a_forward(7)
    product(5, 1, Po)
    finish_two(1)
    scatter(P2, R2, r2_s, r2_r)
    one_ring()
    product(6, 1, Po)
    last_two(0)
    a_ready(7)
    c_send(7)
    product(7, 1, Po)
    last_two(1)
    scatter(P3, R3, r3_s, r3_r)
    one_all()
    gather(P2, R2, G2, r2_r, g2_s, g2_r)
    gather(P3, R3, G3, r3_r, g3_s, g3_r)
    cross_two(2)
    cross_two(3)
    write(1, c2, o2).start()
    tiles_one()
    write(2, d1, od1).start()
    write(3, l2, ol2).start()
    gathered(G2, g2_r)
    gathered(G3, g3_r)
    for s in range(2):
        d2[s] = d2[s] + G2[:, s].reshape(TILE, TILE)
        d2[2 + s] = d2[2 + s] + G3[:, s].reshape(TILE, TILE)
    write(4, d2, od2).start()
    b_spread_done()
    for copy in sends:
        copy.wait_send()
    for i, (src, dst) in enumerate(((c1, o1), (c2, o2), (d1, od1), (l2, ol2), (d2, od2))):
        write(i, src, dst).wait()


def finish(*refs):
    for src, dst in zip(refs[:5], refs[5:]):
        dst[...] = src[...]


def local(
    sigma_sep, factor_one, inverse_one, list_one, factor_two, factor_link, inverse_two, list_two
):
    vmem = pl.BlockSpec(memory_space=pltpu.VMEM)
    wide = jax.ShapeDtypeStruct((SUPERS * TILE, WIDE), F32)
    tiles = jax.ShapeDtypeStruct((SUPERS, TILE, TILE), F32)
    dma = pltpu.SemaphoreType.DMA
    anywhere = pl.BlockSpec(memory_space=pl.ANY)
    made = pl.pallas_call(
        kernel,
        out_shape=(wide, tiles, wide, tiles, tiles),
        in_specs=[anywhere, anywhere, vmem, vmem, anywhere, vmem, vmem, vmem],
        out_specs=(anywhere,) * 5,
        scratch_shapes=[
            pltpu.VMEM((SUPERS * TILE, WIDE), F32),
            pltpu.VMEM((SUPERS, TILE, TILE), F32),
            pltpu.VMEM((SUPERS * TILE, WIDE), F32),
            pltpu.VMEM((SUPERS, TILE, TILE), F32),
            pltpu.VMEM((SUPERS, TILE, TILE), F32),
            pltpu.VMEM((CHUNKS, TILE, WIDE), F32),
            pltpu.VMEM((2, TILE, WIDE), F32),
            pltpu.VMEM((2, SUPERS, WIDE), F32),
            pltpu.VMEM((4, CHUNKS * TILE, WIDE), F32),
            pltpu.VMEM((CHUNKS, 2 * TILE, 4 * WIDE), BF16),
            pltpu.VMEM((2, 4 * WIDE, WIDE), F32),
            pltpu.VMEM((2, 4 * WIDE, WIDE), BF16),
            pltpu.VMEM((2, 4 * WIDE, WIDE), BF16),
            pltpu.VMEM((CHUNKS, TILE, WIDE), F32),
            pltpu.VMEM((CHUNKS, TILE, WIDE), F32),
            pltpu.VMEM((CHUNKS, TILE, WIDE), F32),
            pltpu.VMEM((2, SUPERS, TILE, TILE), F32),
            pltpu.VMEM((SUPERS, TILE, TILE), F32),
            pltpu.VMEM((3, TILE, TILE), F32),
            pltpu.VMEM((2, SUPERS, TILE, TILE), F32),
            pltpu.VMEM((8, 2, 16, TILE), F32),
            pltpu.VMEM((7, 2, 16, TILE), F32),
            pltpu.VMEM((8, 2, 16, TILE), F32),
            pltpu.VMEM((8, 2, 16, TILE), F32),
            pltpu.VMEM((7, 2, 16, TILE), F32),
            pltpu.VMEM((8, 2, 16, TILE), F32),
            pltpu.VMEM((SUPERS, TILE, TILE), F32),
            dma((2, CHUNKS)), dma((2, CHUNKS)), dma((2, CHUNKS)), dma((2, CHUNKS)),
            dma((2, 2)), dma((2, 2)),
            dma((2, 2, 4, 2)), dma((2, 2, 4, 2)),
            dma((2, 2, 5, 2)), dma((2, 2, 5, 2)),
            dma((CHUNKS,)), dma((CHUNKS,)),
            dma, dma, dma((3,)), dma((3,)), dma((7,)), dma((7,)),
            dma((7,)), dma((7,)), dma((7,)), dma((7,)),
            dma((7,)), dma((7,)), dma((7,)), dma((7,)),
            dma((CHUNKS,)), dma((2,)), dma((2,)), dma((5,)),
        ],
        compiler_params=pltpu.CompilerParams(
            collective_id=0, has_side_effects=True, vmem_limit_bytes=60 * 2**20
        ),
        cost_estimate=pl.CostEstimate(
            flops=13_000_000_000, bytes_accessed=8_000_000, transcendentals=0
        ),
    )(sigma_sep, factor_one, inverse_one, list_one, factor_two, factor_link, inverse_two, list_two)
    return pl.pallas_call(
        finish,
        out_shape=(wide, tiles, wide, tiles, tiles),
        in_specs=[vmem] * 5,
        out_specs=(vmem,) * 5,
        compiler_params=pltpu.CompilerParams(vmem_limit_bytes=60 * 2**20),
    )(*made)


def solution(mesh):
    return jax.shard_map(
        local,
        mesh=mesh,
        in_specs=(
            P("col", "row"),
            P("col", "row"),
            P("col", None, None),
            P("col", None),
            P("col", "row"),
            P("col", None, None),
            P("col", None, None),
            P("col", None),
        ),
        out_specs=(
            P("col", "row"),
            P("col", None, None),
            P("col", "row"),
            P("col", None, None),
            P("col", None, None),
        ),
        check_vma=False,
    )
```

```python
import functools

import jax
import jax.numpy as jnp
from jax import lax
from jax.experimental import pallas as pl
from jax.experimental.pallas import tpu as pltpu
from jax.sharding import PartitionSpec as P

TILE = 128
MESH = pl.DeviceIdType.MESH
F32 = jnp.float32
BF16 = jnp.bfloat16
WIDE = 512
SUPERS = 4
CHUNKS = 8


def split(x):
    high = x.astype(BF16)
    low = (x - high.astype(F32)).astype(BF16)
    return high, low


def dot3(a, b, ca, cb):
    ah, al = split(a)
    bh, bl = split(b)
    dg = lambda u, v: lax.dot_general(u, v, (((ca,), (cb,)), ((), ())), preferred_element_type=F32)
    return dg(ah, bh) + (dg(ah, bl) + dg(al, bh))


def kernel(
    sig, f1, i1, n1, f2, fl, i2, n2,
    o1, od1, o2, ol2, od2,
    c1, d1, c2, l2, d2, F, Up, H, A, As, B, Bh, Bl, Cs, Cr, Po, P1, R1, G1, P2, R2, G2, P3, R3, G3, LU,
    as_s, as_r, af_s, af_r, bx_s, bx_r, bz_s, bz_r, bc_s, bc_r, c_s, c_r, r1_s, r1_r, g1_s, g1_r, r2_s, r2_r, g2_s, g2_r,
    r3_s, r3_r, g3_s, g3_r, f_r, u_s, u_r, o_s,
):
    row = lax.axis_index("row")
    col = lax.axis_index("col")
    xl, y = row // 4, row % 4
    xh, z, c = col // 16, (col // 2) % 8, col % 2
    sends = []

    def remote(src, dst, ss, rs, dev):
        return pltpu.make_async_remote_copy(
            src_ref=src, dst_ref=dst, send_sem=ss, recv_sem=rs, device_id=dev, device_id_type=MESH
        )

    def start(*args):
        copy = remote(*args)
        copy.start()
        sends.append(copy)

    def arrived(ref, sem):
        pltpu.make_async_copy(ref, ref, sem).wait()

    right, left = (xl * 4 + (y + 1) % 4, col), (xl * 4 + (y + 3) % 4, col)
    pair = ((1 - xl) * 4 + y, col)
    up, down = (row, xh * 16 + ((z + 1) % 8) * 2 + c), (row, xh * 16 + ((z + 7) % 8) * 2 + c)
    twin = (row, xh * 16 + z * 2 + (1 - c))
    other_col = (1 - xh) * 16 + z * 2 + c
    peers = [((row + i) % 8, col) for i in range(1, 8)]
    barrier = pltpu.get_barrier_semaphore()
    for dev in peers + [up, down, twin, (row, other_col), ((1 - xl) * 4 + y, other_col)]:
        pl.semaphore_signal(barrier, inc=1, device_id=dev, device_id_type=MESH)

    def load(q):
        rows = pl.ds(q % SUPERS * TILE, TILE)
        return pltpu.make_async_copy((f1, f2)[q // SUPERS].at[rows, :], F.at[q], f_r.at[q])

    for q in range(CHUNKS):
        load(q).start()

    for level, lists in enumerate((n1, n2)):
        for t in range(4):
            match = jnp.where(lists[...] == row * 4 + t, 1.0, 0.0).astype(F32)
            mark = jnp.sum(match, axis=1, keepdims=True)
            H[level, :, t * TILE:(t + 1) * TILE] = jnp.broadcast_to(mark, (SUPERS, TILE))

    def hits(level, s):
        return H[level, s:s + 1, :]

    def upper(q):
        level, s = q // SUPERS, q % SUPERS
        inv = (i1, i2)[level]
        load(q).wait()
        masked = F[q, :, :] * hits(level, s)
        A[y, q * TILE:(q + 1) * TILE, :] = dot3(inv[s].T, masked, 1, 0)

    def a_block(slot, first, count):
        return A.at[slot, pl.ds(first, count), :]

    def a_send(q):
        for d, dev in enumerate((right, left)):
            ref = a_block(y, q * TILE, TILE)
            start(ref, ref, as_s.at[d, q], as_r.at[d, q], dev)

    def a_forward(q):
        for d, dev in enumerate((right, left)):
            slot = (y + (3, 1)[d]) % 4
            arrived(a_block(slot, q * TILE, TILE), as_r.at[d, q])
            ref = a_block(slot, q * TILE + d * 64, 64)
            start(ref, ref, af_s.at[d, q], af_r.at[d, q], dev)

    def a_ready(q):
        for d in range(2):
            arrived(a_block((y + 2) % 4, q * TILE + d * 64, 64), af_r.at[d, q])
        for k in range(4):
            high, low = split(A[k, q * TILE:(q + 1) * TILE, :])
            As[q, 0:TILE, k * WIDE:(k + 1) * WIDE] = high
            As[q, TILE:2 * TILE, k * WIDE:(k + 1) * WIDE] = low

    pieces = (4, 2)

    def b_rows(k, zs, core, h):
        size = TILE // pieces[k]
        first = pl.multiple_of(((zs + 8) % 8 * 2 + core) * TILE + h * size, size)
        return B.at[(1 - xl, xl)[k], pl.ds(first, size), :]

    def b_out(k, i, h, colt):
        size = TILE // pieces[k]
        first = pl.multiple_of((z * 2 + c) * TILE + h * size, size)
        src, dst = sig.at[pl.ds(h * size, size), :], B.at[xl, pl.ds(first, size), :]
        return remote(src, dst, bx_s.at[i, h], bx_r.at[k, h], (xh * 4 + y, colt))

    def b_spread(k):
        @pl.when((xl != xh) if k == 0 else (xl == xh))
        def _():
            for h in range(pieces[k]):
                if k == 0:
                    b_out(k, 0, h, z * 2 + c).start()
                    b_out(k, 1, h, 16 + z * 2 + c).start()
                else:
                    size = TILE // pieces[k]
                    src = sig.at[pl.ds(h * size, size), :]
                    pltpu.make_async_copy(src, b_rows(k, z, c, h), bx_r.at[k, h]).start()
                    b_out(k, 0, h, other_col).start()

    def b_spread_done():
        for k in range(2):
            @pl.when((xl != xh) if k == 0 else (xl == xh))
            def _():
                for h in range(pieces[k]):
                    for i in range(2 - k):
                        b_out(k, i, h, other_col).wait_send()

    def b_pass(k, d, s, h):
        ref = b_rows(k, z + (-s, s)[d], c, h)
        start(ref, ref, bz_s.at[k, d, s, h], bz_r.at[k, d, s, h], (up, down)[d])

    def b_twin(k, d, s, h):
        ref = b_rows(k, z + (-s, s)[d], c, h)
        start(ref, ref, bc_s.at[k, d, s, h], bc_r.at[k, d, s, h], twin)

    def b_home(k):
        for h in range(pieces[k]):
            arrived(b_rows(k, z, c, h), bx_r.at[k, h])
            b_pass(k, 0, 0, h)
            b_pass(k, 1, 0, h)
            b_twin(k, 0, 0, h)

    def b_step(k, s, h):
        for d in range(2):
            arrived(b_rows(k, z + (-s, s)[d], c, h), bz_r.at[k, d, s - 1, h])
            if s < 3 or h * 2 // pieces[k] == d:
                b_pass(k, d, s, h)
            b_twin(k, d, s, h)

    def b_last(k):
        for h in range(pieces[k]):
            d = h * 2 // pieces[k]
            arrived(b_rows(k, z + 4, c, h), bz_r.at[k, d, 3, h])
            b_twin(k, d, 4, h)
        for h in range(pieces[k]):
            arrived(b_rows(k, z, 1 - c, h), bc_r.at[k, 0, 0, h])
            for d in range(2):
                for s in range(1, 4):
                    arrived(b_rows(k, z + (-s, s)[d], 1 - c, h), bc_r.at[k, d, s, h])
            arrived(b_rows(k, z + 4, 1 - c, h), bc_r.at[k, h * 2 // pieces[k], 4, h])
        which = (1 - xl, xl)[k]

        def cut(i, carry):
            rows = pl.ds(pl.multiple_of(i * TILE, TILE), TILE)
            high, low = split(B[which, rows, :])
            Bh[which, rows, :] = high
            Bl[which, rows, :] = low
            return carry

        lax.fori_loop(0, 16, cut, 0)

    def product(q, k, out):
        which = (1 - xl, xl)[k]
        total = None
        for step in range(4):
            ks = slice(step * WIDE, (step + 1) * WIDE)
            both = jnp.dot(As[q, :, ks], Bh[which, ks, :], preferred_element_type=F32)
            rest = jnp.dot(As[q, 0:TILE, ks], Bl[which, ks, :], preferred_element_type=F32)
            term = both[0:TILE] + (both[TILE:2 * TILE] + rest)
            total = term if total is None else total + term
        out[q, :, :] = total

    def c_send(q):
        product(q, 0, Cs)
        c_start(q)

    def c_start(q):
        start(Cs.at[q], Cr.at[q], c_s.at[q], c_r.at[q], pair)

    def own_upper(q):
        return A[y, q * TILE:(q + 1) * TILE, :]

    def finish_one(s):
        arrived(Cr.at[s], c_r.at[s])
        prod = Po[s] + Cr[s]
        cross = -(hits(0, s) * prod)
        c1[s * TILE:(s + 1) * TILE, :] = cross
        P1[s, 0] = dot3(own_upper(s), prod, 1, 1)
        P1[s, 1] = dot3(cross, own_upper(SUPERS + s), 1, 1)

    def linked(s):
        q = SUPERS + s
        Po[q] = Po[q] + dot3(LU[s], c1[s * TILE:(s + 1) * TILE, :], 1, 0)

    def cross_two(s):
        q = SUPERS + s
        arrived(Cr.at[q], c_r.at[q])
        prod = Po[q] + Cr[q]
        c2[s * TILE:(s + 1) * TILE, :] = -(hits(1, s) * prod)
        return prod

    def finish_two(s):
        linked(s)
        part = dot3(own_upper(SUPERS + s), cross_two(s), 1, 1)
        P2[2 * s] = part[0:64]
        P2[2 * s + 1] = part[64:TILE]

    def send_upper(i):
        start(A.at[y, pl.ds((6 + i) * TILE, TILE), :], Up.at[i], u_s.at[i], u_r.at[i], pair)

    def last_two(i):
        linked(2 + i)
        arrived(Up.at[i], u_r.at[i])
        part = dot3(own_upper(6 + i), Po[6 + i], 1, 1) + dot3(Up[i], Cs[6 + i], 1, 1)
        P3[:, i] = part.reshape(8, 16, TILE)

    def ring_sum(part, got, ss, rs):
        for i in range(3):
            to = (y + i + 1) % 4
            start(part.at[to], got.at[i], ss.at[i], rs.at[i], (xl * 4 + to, col))

    def pair_sum(part, got, ss, rs):
        total = part[y]
        for i in range(3):
            arrived(got.at[i], rs.at[i])
            total = total + got[i]
        got[3] = total
        start(got.at[3], got.at[4], ss.at[3], rs.at[3], pair)

    def ring_all(got, whole, rs, ss, ws):
        arrived(got.at[4], rs.at[3])
        whole[y] = got[3] + got[4]
        for i in range(3):
            start(whole.at[y], whole.at[y], ss.at[i], ws.at[i], (xl * 4 + (y + i + 1) % 4, col))

    def ring_here(whole, ws):
        for i in range(3):
            arrived(whole.at[(y + 3 - i) % 4], ws.at[i])

    def scatter(part, got, ss, rs):
        for i, dev in enumerate(peers):
            start(part.at[dev[0]], got.at[i], ss.at[i], rs.at[i], dev)

    def gather(part, got, whole, waits, ss, rs):
        total = part[row]
        for i in range(7):
            arrived(got.at[i], waits.at[i])
            total = total + got[i]
        whole[row] = total
        for i, dev in enumerate(peers):
            start(whole.at[row], whole.at[row], ss.at[i], rs.at[i], dev)

    def gathered(whole, waits):
        for i in range(7):
            arrived(whole.at[(row + 7 - i) % 8], waits.at[i])

    def side():
        for s in range(SUPERS):
            t1, t2 = i1[s].T, i2[s].T
            LU[s] = dot3(t2, fl[s], 1, 1)
            d1[s] = dot3(t1, t1, 1, 1)
            d2[s] = dot3(t2, t2, 1, 1)

    def tiles_one():
        ring_here(G1, g1_r)
        for s in range(SUPERS):
            diag = d1[s] + G1[s, 0]
            d1[s] = diag
            link = G1[s, 1] + dot3(diag, LU[s], 1, 1)
            l2[s] = -link
            d2[s] = d2[s] + dot3(LU[s], link, 1, 0)

    def write(i, src, dst):
        return pltpu.make_async_copy(src, dst, o_s.at[i])

    upper(0)
    pl.semaphore_wait(barrier, 12)
    a_send(0)
    b_spread(0)
    upper(1)
    a_send(1)
    upper(2)
    a_send(2)
    upper(3)
    b_home(0)
    b_spread(1)
    upper(7)
    send_upper(1)
    upper(4)
    a_forward(0)
    a_send(3)
    for h in range(4):
        b_step(0, 1, h)
    upper(5)
    upper(6)
    send_upper(0)
    a_forward(1)
    a_send(4)
    for h in range(4):
        b_step(0, 2, h)
    side()
    b_step(0, 3, 0)
    b_step(0, 3, 1)
    a_forward(2)
    a_send(5)
    b_step(0, 3, 2)
    b_step(0, 3, 3)
    b_home(1)
    b_last(0)
    a_ready(0)
    c_send(0)
    a_forward(3)
    a_send(6)
    a_ready(1)
    b_step(1, 1, 0)
    c_send(1)
    b_step(1, 1, 1)
    a_ready(2)
    c_send(2)
    b_step(1, 2, 0)
    a_forward(4)
    a_send(7)
    b_step(1, 2, 1)
    a_ready(3)
    c_send(3)
    b_step(1, 3, 0)
    b_step(1, 3, 1)
    a_ready(4)
    c_send(4)
    a_forward(5)
    b_last(1)
    product(0, 1, Po)
    a_ready(5)
    c_send(5)
    finish_one(0)
    product(1, 1, Po)
    finish_one(1)
    a_forward(6)
    product(2, 1, Po)
    finish_one(2)
    product(3, 1, Po)
    finish_one(3)
    ring_sum(P1, R1, r1_s, r1_r)
    write(0, c1, o1).start()
    a_ready(6)
    c_send(6)
    product(4, 1, Po)
    finish_two(0)
    pair_sum(P1, R1, r1_s, r1_r)
    a_forward(7)
    product(5, 1, Po)
    finish_two(1)
    ring_sum(P2, R2, r2_s, r2_r)
    product(6, 1, Po)
    last_two(0)
    a_ready(7)
    product(7, 0, Cs)
    product(7, 1, Po)
    last_two(1)
    scatter(P3, R3, r3_s, r3_r)
    ring_all(R1, G1, r1_r, g1_s, g1_r)
    c_start(7)
    pair_sum(P2, R2, r2_s, r2_r)
    gather(P3, R3, G3, r3_r, g3_s, g3_r)
    ring_all(R2, G2, r2_r, g2_s, g2_r)
    cross_two(2)
    cross_two(3)
    write(1, c2, o2).start()
    tiles_one()
    write(2, d1, od1).start()
    write(3, l2, ol2).start()
    ring_here(G2, g2_r)
    gathered(G3, g3_r)
    for s in range(2):
        d2[s, 0:64] = d2[s, 0:64] + G2[2 * s]
        d2[s, 64:TILE] = d2[s, 64:TILE] + G2[2 * s + 1]
        d2[2 + s] = d2[2 + s] + G3[:, s].reshape(TILE, TILE)
    write(4, d2, od2).start()
    b_spread_done()
    for copy in sends:
        copy.wait_send()
    for i, (src, dst) in enumerate(((c1, o1), (c2, o2), (d1, od1), (l2, ol2), (d2, od2))):
        write(i, src, dst).wait()


def finish(*refs):
    for src, dst in zip(refs[:5], refs[5:]):
        dst[...] = src[...]


def local(
    sigma_sep, factor_one, inverse_one, list_one, factor_two, factor_link, inverse_two, list_two
):
    vmem = pl.BlockSpec(memory_space=pltpu.VMEM)
    wide = jax.ShapeDtypeStruct((SUPERS * TILE, WIDE), F32)
    tiles = jax.ShapeDtypeStruct((SUPERS, TILE, TILE), F32)
    dma = pltpu.SemaphoreType.DMA
    anywhere = pl.BlockSpec(memory_space=pl.ANY)
    made = pl.pallas_call(
        kernel,
        out_shape=(wide, tiles, wide, tiles, tiles),
        in_specs=[anywhere, anywhere, vmem, vmem, anywhere, vmem, vmem, vmem],
        out_specs=(anywhere,) * 5,
        scratch_shapes=[
            pltpu.VMEM((SUPERS * TILE, WIDE), F32),
            pltpu.VMEM((SUPERS, TILE, TILE), F32),
            pltpu.VMEM((SUPERS * TILE, WIDE), F32),
            pltpu.VMEM((SUPERS, TILE, TILE), F32),
            pltpu.VMEM((SUPERS, TILE, TILE), F32),
            pltpu.VMEM((CHUNKS, TILE, WIDE), F32),
            pltpu.VMEM((2, TILE, WIDE), F32),
            pltpu.VMEM((2, SUPERS, WIDE), F32),
            pltpu.VMEM((4, CHUNKS * TILE, WIDE), F32),
            pltpu.VMEM((CHUNKS, 2 * TILE, 4 * WIDE), BF16),
            pltpu.VMEM((2, 4 * WIDE, WIDE), F32),
            pltpu.VMEM((2, 4 * WIDE, WIDE), BF16),
            pltpu.VMEM((2, 4 * WIDE, WIDE), BF16),
            pltpu.VMEM((CHUNKS, TILE, WIDE), F32),
            pltpu.VMEM((CHUNKS, TILE, WIDE), F32),
            pltpu.VMEM((CHUNKS, TILE, WIDE), F32),
            pltpu.VMEM((SUPERS, 2, TILE, TILE), F32),
            pltpu.VMEM((5, 2, TILE, TILE), F32),
            pltpu.VMEM((SUPERS, 2, TILE, TILE), F32),
            pltpu.VMEM((4, 64, TILE), F32),
            pltpu.VMEM((5, 64, TILE), F32),
            pltpu.VMEM((4, 64, TILE), F32),
            pltpu.VMEM((8, 2, 16, TILE), F32),
            pltpu.VMEM((7, 2, 16, TILE), F32),
            pltpu.VMEM((8, 2, 16, TILE), F32),
            pltpu.VMEM((SUPERS, TILE, TILE), F32),
            dma((2, CHUNKS)), dma((2, CHUNKS)), dma((2, CHUNKS)), dma((2, CHUNKS)),
            dma((2, 4)), dma((2, 4)),
            dma((2, 2, 4, 4)), dma((2, 2, 4, 4)),
            dma((2, 2, 5, 4)), dma((2, 2, 5, 4)),
            dma((CHUNKS,)), dma((CHUNKS,)),
            dma((4,)), dma((4,)), dma((3,)), dma((3,)),
            dma((4,)), dma((4,)), dma((3,)), dma((3,)),
            dma((7,)), dma((7,)), dma((7,)), dma((7,)),
            dma((CHUNKS,)), dma((2,)), dma((2,)), dma((5,)),
        ],
        compiler_params=pltpu.CompilerParams(
            collective_id=0, has_side_effects=True, vmem_limit_bytes=60 * 2**20
        ),
        cost_estimate=pl.CostEstimate(
            flops=13_000_000_000, bytes_accessed=8_000_000, transcendentals=0
        ),
    )(sigma_sep, factor_one, inverse_one, list_one, factor_two, factor_link, inverse_two, list_two)
    return pl.pallas_call(
        finish,
        out_shape=(wide, tiles, wide, tiles, tiles),
        in_specs=[vmem] * 5,
        out_specs=(vmem,) * 5,
        compiler_params=pltpu.CompilerParams(vmem_limit_bytes=60 * 2**20),
    )(*made)


def solution(mesh):
    return jax.shard_map(
        local,
        mesh=mesh,
        in_specs=(
            P("col", "row"),
            P("col", "row"),
            P("col", None, None),
            P("col", None),
            P("col", "row"),
            P("col", None, None),
            P("col", None, None),
            P("col", None),
        ),
        out_specs=(
            P("col", "row"),
            P("col", None, None),
            P("col", "row"),
            P("col", None, None),
            P("col", None, None),
        ),
        check_vma=False,
    )
```

```python
import functools

import jax
import jax.numpy as jnp
from jax import lax
from jax.experimental import pallas as pl
from jax.experimental.pallas import tpu as pltpu
from jax.sharding import PartitionSpec as P

TILE = 128
MESH = pl.DeviceIdType.MESH
F32 = jnp.float32
BF16 = jnp.bfloat16
WIDE = 512
SUPERS = 4
CHUNKS = 8


def split(x):
    high = x.astype(BF16)
    low = (x - high.astype(F32)).astype(BF16)
    return high, low


def dot3(a, b, ca, cb):
    ah, al = split(a)
    bh, bl = split(b)
    dg = lambda u, v: lax.dot_general(u, v, (((ca,), (cb,)), ((), ())), preferred_element_type=F32)
    return dg(ah, bh) + (dg(ah, bl) + dg(al, bh))


def kernel(
    sig, f1, i1, n1, f2, fl, i2, n2,
    o1, od1, o2, ol2, od2,
    c1, d1, c2, l2, d2, F, Up, H, A, As, B, Bh, Bl, Cs, Cr, Po, P1, R1, G1, P2, R2, G2, P3, R3, G3, LU,
    as_s, as_r, af_s, af_r, bx_s, bx_r, bz_s, bz_r, bc_s, bc_r, c_s, c_r, r1_s, r1_r, g1_s, g1_r, r2_s, r2_r, g2_s, g2_r,
    r3_s, r3_r, g3_s, g3_r, f_r, u_s, u_r, o_s,
):
    row = lax.axis_index("row")
    col = lax.axis_index("col")
    xl, y = row // 4, row % 4
    xh, z, c = col // 16, (col // 2) % 8, col % 2
    sends = []

    def remote(src, dst, ss, rs, dev):
        return pltpu.make_async_remote_copy(
            src_ref=src, dst_ref=dst, send_sem=ss, recv_sem=rs, device_id=dev, device_id_type=MESH
        )

    def start(*args):
        copy = remote(*args)
        copy.start()
        sends.append(copy)

    def arrived(ref, sem):
        pltpu.make_async_copy(ref, ref, sem).wait()

    right, left = (xl * 4 + (y + 1) % 4, col), (xl * 4 + (y + 3) % 4, col)
    pair = ((1 - xl) * 4 + y, col)
    up, down = (row, xh * 16 + ((z + 1) % 8) * 2 + c), (row, xh * 16 + ((z + 7) % 8) * 2 + c)
    twin = (row, xh * 16 + z * 2 + (1 - c))
    other_col = (1 - xh) * 16 + z * 2 + c
    peers = [((row + i) % 8, col) for i in range(1, 8)]
    barrier = pltpu.get_barrier_semaphore()
    for dev in peers + [up, down, twin, (row, other_col), ((1 - xl) * 4 + y, other_col)]:
        pl.semaphore_signal(barrier, inc=1, device_id=dev, device_id_type=MESH)

    def load(q):
        rows = pl.ds(q % SUPERS * TILE, TILE)
        return pltpu.make_async_copy((f1, f2)[q // SUPERS].at[rows, :], F.at[q], f_r.at[q])

    for q in range(CHUNKS):
        load(q).start()

    for level, lists in enumerate((n1, n2)):
        for t in range(4):
            match = jnp.where(lists[...] == row * 4 + t, 1.0, 0.0).astype(F32)
            mark = jnp.sum(match, axis=1, keepdims=True)
            H[level, :, t * TILE:(t + 1) * TILE] = jnp.broadcast_to(mark, (SUPERS, TILE))

    def hits(level, s):
        return H[level, s:s + 1, :]

    def upper(q):
        level, s = q // SUPERS, q % SUPERS
        inv = (i1, i2)[level]
        load(q).wait()
        masked = F[q, :, :] * hits(level, s)
        A[y, q * TILE:(q + 1) * TILE, :] = dot3(inv[s].T, masked, 1, 0)

    def a_block(slot, first, count):
        return A.at[slot, pl.ds(first, count), :]

    def a_send(q):
        for d, dev in enumerate((right, left)):
            ref = a_block(y, q * TILE, TILE)
            start(ref, ref, as_s.at[d, q], as_r.at[d, q], dev)

    def a_forward(q):
        for d, dev in enumerate((right, left)):
            slot = (y + (3, 1)[d]) % 4
            arrived(a_block(slot, q * TILE, TILE), as_r.at[d, q])
            ref = a_block(slot, q * TILE + d * 64, 64)
            start(ref, ref, af_s.at[d, q], af_r.at[d, q], dev)

    def a_ready(q):
        for d in range(2):
            arrived(a_block((y + 2) % 4, q * TILE + d * 64, 64), af_r.at[d, q])
        for k in range(4):
            high, low = split(A[k, q * TILE:(q + 1) * TILE, :])
            As[q, 0:TILE, k * WIDE:(k + 1) * WIDE] = high
            As[q, TILE:2 * TILE, k * WIDE:(k + 1) * WIDE] = low

    pieces = (4, 2)

    def b_rows(k, zs, core, h):
        size = TILE // pieces[k]
        first = pl.multiple_of(((zs + 8) % 8 * 2 + core) * TILE + h * size, size)
        return B.at[(1 - xl, xl)[k], pl.ds(first, size), :]

    def b_out(k, i, h, colt):
        size = TILE // pieces[k]
        first = pl.multiple_of((z * 2 + c) * TILE + h * size, size)
        src, dst = sig.at[pl.ds(h * size, size), :], B.at[xl, pl.ds(first, size), :]
        return remote(src, dst, bx_s.at[i, h], bx_r.at[k, h], (xh * 4 + y, colt))

    def b_spread(k):
        @pl.when((xl != xh) if k == 0 else (xl == xh))
        def _():
            for h in range(pieces[k]):
                if k == 0:
                    b_out(k, 0, h, z * 2 + c).start()
                    b_out(k, 1, h, 16 + z * 2 + c).start()
                else:
                    size = TILE // pieces[k]
                    src = sig.at[pl.ds(h * size, size), :]
                    pltpu.make_async_copy(src, b_rows(k, z, c, h), bx_r.at[k, h]).start()
                    b_out(k, 0, h, other_col).start()

    def b_spread_done():
        for k in range(2):
            @pl.when((xl != xh) if k == 0 else (xl == xh))
            def _():
                for h in range(pieces[k]):
                    for i in range(2 - k):
                        b_out(k, i, h, other_col).wait_send()

    def b_pass(k, d, s, h):
        ref = b_rows(k, z + (-s, s)[d], c, h)
        start(ref, ref, bz_s.at[k, d, s, h], bz_r.at[k, d, s, h], (up, down)[d])

    def b_twin(k, d, s, h):
        ref = b_rows(k, z + (-s, s)[d], c, h)
        start(ref, ref, bc_s.at[k, d, s, h], bc_r.at[k, d, s, h], twin)

    def b_home(k):
        for h in range(pieces[k]):
            arrived(b_rows(k, z, c, h), bx_r.at[k, h])
            b_pass(k, 0, 0, h)
            b_pass(k, 1, 0, h)
            b_twin(k, 0, 0, h)

    def b_step(k, s, h):
        for d in range(2):
            arrived(b_rows(k, z + (-s, s)[d], c, h), bz_r.at[k, d, s - 1, h])
            if s < 3 or h * 2 // pieces[k] == d:
                b_pass(k, d, s, h)
            b_twin(k, d, s, h)

    def b_last(k):
        for h in range(pieces[k]):
            d = h * 2 // pieces[k]
            arrived(b_rows(k, z + 4, c, h), bz_r.at[k, d, 3, h])
            b_twin(k, d, 4, h)
        for h in range(pieces[k]):
            arrived(b_rows(k, z, 1 - c, h), bc_r.at[k, 0, 0, h])
            for d in range(2):
                for s in range(1, 4):
                    arrived(b_rows(k, z + (-s, s)[d], 1 - c, h), bc_r.at[k, d, s, h])
            arrived(b_rows(k, z + 4, 1 - c, h), bc_r.at[k, h * 2 // pieces[k], 4, h])
        which = (1 - xl, xl)[k]

        def cut(i, carry):
            rows = pl.ds(pl.multiple_of(i * TILE, TILE), TILE)
            high, low = split(B[which, rows, :])
            Bh[which, rows, :] = high
            Bl[which, rows, :] = low
            return carry

        lax.fori_loop(0, 16, cut, 0)

    def product(q, k, out):
        which = (1 - xl, xl)[k]
        total = None
        for step in range(4):
            ks = slice(step * WIDE, (step + 1) * WIDE)
            both = jnp.dot(As[q, :, ks], Bh[which, ks, :], preferred_element_type=F32)
            rest = jnp.dot(As[q, 0:TILE, ks], Bl[which, ks, :], preferred_element_type=F32)
            term = both[0:TILE] + (both[TILE:2 * TILE] + rest)
            total = term if total is None else total + term
        out[q, :, :] = total

    def c_send(q):
        product(q, 0, Cs)
        c_start(q)

    def c_start(q):
        start(Cs.at[q], Cr.at[q], c_s.at[q], c_r.at[q], pair)

    def own_upper(q):
        return A[y, q * TILE:(q + 1) * TILE, :]

    def finish_one(s):
        arrived(Cr.at[s], c_r.at[s])
        prod = Po[s] + Cr[s]
        cross = -(hits(0, s) * prod)
        c1[s * TILE:(s + 1) * TILE, :] = cross
        P1[s, 0] = dot3(own_upper(s), prod, 1, 1)
        P1[s, 1] = dot3(cross, own_upper(SUPERS + s), 1, 1)

    def linked(s):
        q = SUPERS + s
        Po[q] = Po[q] + dot3(LU[s], c1[s * TILE:(s + 1) * TILE, :], 1, 0)

    def cross_two(s):
        q = SUPERS + s
        arrived(Cr.at[q], c_r.at[q])
        prod = Po[q] + Cr[q]
        c2[s * TILE:(s + 1) * TILE, :] = -(hits(1, s) * prod)
        return prod

    def finish_two(s):
        linked(s)
        part = dot3(own_upper(SUPERS + s), cross_two(s), 1, 1)
        P2[2 * s] = part[0:64]
        P2[2 * s + 1] = part[64:TILE]

    def send_upper(i):
        start(A.at[y, pl.ds((6 + i) * TILE, TILE), :], Up.at[i], u_s.at[i], u_r.at[i], pair)

    def last_two(i):
        linked(2 + i)
        arrived(Up.at[i], u_r.at[i])
        part = dot3(own_upper(6 + i), Po[6 + i], 1, 1) + dot3(Up[i], Cs[6 + i], 1, 1)
        P3[:, i] = part.reshape(8, 16, TILE)

    def ring_sum(part, got, ss, rs):
        for i in range(3):
            to = (y + i + 1) % 4
            start(part.at[to], got.at[i], ss.at[i], rs.at[i], (xl * 4 + to, col))

    def pair_sum(part, got, ss, rs):
        total = part[y]
        for i in range(3):
            arrived(got.at[i], rs.at[i])
            total = total + got[i]
        got[3] = total
        start(got.at[3], got.at[4], ss.at[3], rs.at[3], pair)

    def ring_all(got, whole, rs, ss, ws):
        arrived(got.at[4], rs.at[3])
        whole[y] = got[3] + got[4]
        for i in range(3):
            start(whole.at[y], whole.at[y], ss.at[i], ws.at[i], (xl * 4 + (y + i + 1) % 4, col))

    def ring_here(whole, ws):
        for i in range(3):
            arrived(whole.at[(y + 3 - i) % 4], ws.at[i])

    def scatter(part, got, ss, rs):
        for i, dev in enumerate(peers):
            start(part.at[dev[0]], got.at[i], ss.at[i], rs.at[i], dev)

    def gather(part, got, whole, waits, ss, rs):
        total = part[row]
        for i in range(7):
            arrived(got.at[i], waits.at[i])
            total = total + got[i]
        whole[row] = total
        for i, dev in enumerate(peers):
            start(whole.at[row], whole.at[row], ss.at[i], rs.at[i], dev)

    def gathered(whole, waits):
        for i in range(7):
            arrived(whole.at[(row + 7 - i) % 8], waits.at[i])

    def side():
        for s in range(SUPERS):
            t1, t2 = i1[s].T, i2[s].T
            LU[s] = dot3(t2, fl[s], 1, 1)
            d1[s] = dot3(t1, t1, 1, 1)
            d2[s] = dot3(t2, t2, 1, 1)

    def tiles_one():
        ring_here(G1, g1_r)
        for s in range(SUPERS):
            diag = d1[s] + G1[s, 0]
            d1[s] = diag
            link = G1[s, 1] + dot3(diag, LU[s], 1, 1)
            l2[s] = -link
            d2[s] = d2[s] + dot3(LU[s], link, 1, 0)

    def write(i, src, dst):
        return pltpu.make_async_copy(src, dst, o_s.at[i])

    upper(0)
    pl.semaphore_wait(barrier, 12)
    a_send(0)
    b_spread(0)
    upper(1)
    a_send(1)
    upper(2)
    a_send(2)
    upper(3)
    b_home(0)
    b_spread(1)
    upper(7)
    send_upper(1)
    upper(4)
    a_forward(0)
    a_send(3)
    for h in range(4):
        b_step(0, 1, h)
    upper(5)
    upper(6)
    send_upper(0)
    a_forward(1)
    a_send(4)
    for h in range(4):
        b_step(0, 2, h)
    side()
    b_step(0, 3, 0)
    b_step(0, 3, 1)
    a_forward(2)
    a_send(5)
    b_step(0, 3, 2)
    b_step(0, 3, 3)
    b_home(1)
    b_last(0)
    a_ready(0)
    c_send(0)
    a_forward(3)
    a_send(6)
    a_ready(1)
    b_step(1, 1, 0)
    c_send(1)
    b_step(1, 1, 1)
    a_ready(2)
    c_send(2)
    b_step(1, 2, 0)
    a_forward(4)
    a_send(7)
    b_step(1, 2, 1)
    a_ready(3)
    c_send(3)
    b_step(1, 3, 0)
    b_step(1, 3, 1)
    a_ready(4)
    c_send(4)
    a_forward(5)
    b_last(1)
    a_ready(5)
    c_send(5)
    a_forward(6)
    for s in range(4):
        product(s, 1, Po)
        finish_one(s)
        if s == 2:
            a_forward(7)
    ring_sum(P1, R1, r1_s, r1_r)
    a_ready(6)
    c_send(6)
    write(0, c1, o1).start()
    product(4, 1, Po)
    finish_two(0)
    product(5, 1, Po)
    finish_two(1)
    ring_sum(P2, R2, r2_s, r2_r)
    product(6, 1, Po)
    last_two(0)
    pair_sum(P1, R1, r1_s, r1_r)
    a_ready(7)
    product(7, 0, Cs)
    product(7, 1, Po)
    last_two(1)
    scatter(P3, R3, r3_s, r3_r)
    ring_all(R1, G1, r1_r, g1_s, g1_r)
    c_start(7)
    pair_sum(P2, R2, r2_s, r2_r)
    gather(P3, R3, G3, r3_r, g3_s, g3_r)
    ring_all(R2, G2, r2_r, g2_s, g2_r)
    cross_two(2)
    cross_two(3)
    write(1, c2, o2).start()
    tiles_one()
    write(2, d1, od1).start()
    write(3, l2, ol2).start()
    ring_here(G2, g2_r)
    gathered(G3, g3_r)
    for s in range(2):
        d2[s, 0:64] = d2[s, 0:64] + G2[2 * s]
        d2[s, 64:TILE] = d2[s, 64:TILE] + G2[2 * s + 1]
        d2[2 + s] = d2[2 + s] + G3[:, s].reshape(TILE, TILE)
    write(4, d2, od2).start()
    b_spread_done()
    for copy in sends:
        copy.wait_send()
    for i, (src, dst) in enumerate(((c1, o1), (c2, o2), (d1, od1), (l2, ol2), (d2, od2))):
        write(i, src, dst).wait()


def finish(*refs):
    for src, dst in zip(refs[:5], refs[5:]):
        dst[...] = src[...]


def local(
    sigma_sep, factor_one, inverse_one, list_one, factor_two, factor_link, inverse_two, list_two
):
    vmem = pl.BlockSpec(memory_space=pltpu.VMEM)
    wide = jax.ShapeDtypeStruct((SUPERS * TILE, WIDE), F32)
    tiles = jax.ShapeDtypeStruct((SUPERS, TILE, TILE), F32)
    dma = pltpu.SemaphoreType.DMA
    anywhere = pl.BlockSpec(memory_space=pl.ANY)
    made = pl.pallas_call(
        kernel,
        out_shape=(wide, tiles, wide, tiles, tiles),
        in_specs=[anywhere, anywhere, vmem, vmem, anywhere, vmem, vmem, vmem],
        out_specs=(anywhere,) * 5,
        scratch_shapes=[
            pltpu.VMEM((SUPERS * TILE, WIDE), F32),
            pltpu.VMEM((SUPERS, TILE, TILE), F32),
            pltpu.VMEM((SUPERS * TILE, WIDE), F32),
            pltpu.VMEM((SUPERS, TILE, TILE), F32),
            pltpu.VMEM((SUPERS, TILE, TILE), F32),
            pltpu.VMEM((CHUNKS, TILE, WIDE), F32),
            pltpu.VMEM((2, TILE, WIDE), F32),
            pltpu.VMEM((2, SUPERS, WIDE), F32),
            pltpu.VMEM((4, CHUNKS * TILE, WIDE), F32),
            pltpu.VMEM((CHUNKS, 2 * TILE, 4 * WIDE), BF16),
            pltpu.VMEM((2, 4 * WIDE, WIDE), F32),
            pltpu.VMEM((2, 4 * WIDE, WIDE), BF16),
            pltpu.VMEM((2, 4 * WIDE, WIDE), BF16),
            pltpu.VMEM((CHUNKS, TILE, WIDE), F32),
            pltpu.VMEM((CHUNKS, TILE, WIDE), F32),
            pltpu.VMEM((CHUNKS, TILE, WIDE), F32),
            pltpu.VMEM((SUPERS, 2, TILE, TILE), F32),
            pltpu.VMEM((5, 2, TILE, TILE), F32),
            pltpu.VMEM((SUPERS, 2, TILE, TILE), F32),
            pltpu.VMEM((4, 64, TILE), F32),
            pltpu.VMEM((5, 64, TILE), F32),
            pltpu.VMEM((4, 64, TILE), F32),
            pltpu.VMEM((8, 2, 16, TILE), F32),
            pltpu.VMEM((7, 2, 16, TILE), F32),
            pltpu.VMEM((8, 2, 16, TILE), F32),
            pltpu.VMEM((SUPERS, TILE, TILE), F32),
            dma((2, CHUNKS)), dma((2, CHUNKS)), dma((2, CHUNKS)), dma((2, CHUNKS)),
            dma((2, 4)), dma((2, 4)),
            dma((2, 2, 4, 4)), dma((2, 2, 4, 4)),
            dma((2, 2, 5, 4)), dma((2, 2, 5, 4)),
            dma((CHUNKS,)), dma((CHUNKS,)),
            dma((4,)), dma((4,)), dma((3,)), dma((3,)),
            dma((4,)), dma((4,)), dma((3,)), dma((3,)),
            dma((7,)), dma((7,)), dma((7,)), dma((7,)),
            dma((CHUNKS,)), dma((2,)), dma((2,)), dma((5,)),
        ],
        compiler_params=pltpu.CompilerParams(
            collective_id=0, has_side_effects=True, vmem_limit_bytes=60 * 2**20
        ),
        cost_estimate=pl.CostEstimate(
            flops=13_000_000_000, bytes_accessed=8_000_000, transcendentals=0
        ),
    )(sigma_sep, factor_one, inverse_one, list_one, factor_two, factor_link, inverse_two, list_two)
    return pl.pallas_call(
        finish,
        out_shape=(wide, tiles, wide, tiles, tiles),
        in_specs=[vmem] * 5,
        out_specs=(vmem,) * 5,
        compiler_params=pltpu.CompilerParams(vmem_limit_bytes=60 * 2**20),
    )(*made)


def solution(mesh):
    return jax.shard_map(
        local,
        mesh=mesh,
        in_specs=(
            P("col", "row"),
            P("col", "row"),
            P("col", None, None),
            P("col", None),
            P("col", "row"),
            P("col", None, None),
            P("col", None, None),
            P("col", None),
        ),
        out_specs=(
            P("col", "row"),
            P("col", None, None),
            P("col", "row"),
            P("col", None, None),
            P("col", None, None),
        ),
        check_vma=False,
    )
```
